256 devices in a mesh: row: 16 (over z_lo, y, core), col: 16 (over z_hi, x).
Axes of the slice: x: 4, y: 4, z: 8 (z_hi: 4, z_lo: 2; z = z_hi * 2 + z_lo), core: 2. Of those that a mesh axis runs over, the one named last changes fastest.
Arguments:
- expression: bfloat16 [65536, 256], P(('row', 'col')), may hold values from -32 to 32
- panel_index: int32 [1], replicated, may hold values from 0 to 511
Outputs:
- scaled_degree: float32 [65536], P(('row', 'col'))
- correlation: float32 [65536, 128], P(('row', 'col'))
The draws below stay inside these ranges and needn't reach their ends.
All inputs are finite; a program needn't handle non-finite values.
Results may differ from the reference program's by a relative error of at most 0.003.
Values may be sent and summed in bfloat16 or wider, within the bound.
No kernel may reach another device: no remote copies, remote signals or barrier semaphores. Data moves between devices by JAX's collectives and lax.ppermute only.
A program may use at most 64 MiB of HBM per device.

```python
import math
import jax
import jax.numpy as jnp
from jax import lax

GENES = 65536
SAMPLES = 256
PANEL = 128
STRETCH = 256
BLOCK_COLS = 4096


def draw_expression(key, part):
    key = jax.random.fold_in(key, 11)
    keys = jax.random.split(key, 11)
    columns = GENES // BLOCK_COLS
    half_cols = columns // 2
    spread_modules = GENES // 1024
    paired_per = 4
    modules = spread_modules + paired_per * half_cols
    factors = jnp.clip(jax.random.normal(keys[0], (modules, SAMPLES), jnp.float32), -5.0, 5.0)
    programs = jnp.clip(jax.random.normal(keys[7], (4, SAMPLES), jnp.float32), -5.0, 5.0)
    genes = jnp.arange(GENES, dtype=jnp.int32)
    family = genes // STRETCH % columns % half_cols
    paired_member = spread_modules + family * paired_per + jax.random.randint(keys[9], (GENES,), 0, paired_per)
    spread_member = jax.random.randint(keys[1], (GENES,), 0, spread_modules)
    is_paired = jax.random.bernoulli(keys[10], 0.5, (GENES,))
    member = jnp.where(is_paired, paired_member, spread_member)
    load = jax.random.uniform(keys[2], (GENES, 1), jnp.float32, 0.5, 0.9)
    common_load = jax.random.uniform(keys[8], (GENES, 4), jnp.float32, 0.15, 0.35)
    sign = jnp.where(jax.random.bernoulli(keys[3], 0.5, (GENES, 1)), 1.0, -1.0)
    noise = jnp.clip(jax.random.normal(keys[4], (GENES, SAMPLES), jnp.float32), -5.0, 5.0)
    common_part = common_load[:, 0:1] * programs[0][None, :]
    common_part = common_part + common_load[:, 1:2] * programs[1][None, :]
    common_part = common_part + common_load[:, 2:3] * programs[2][None, :]
    common_part = common_part + common_load[:, 3:4] * programs[3][None, :]
    scale = jnp.exp(jax.random.uniform(keys[5], (GENES, 1), jnp.float32, 0.0, math.log(10.0)))
    center = jax.random.uniform(keys[6], (GENES, 1), jnp.float32, -3.0, 3.0)
    signal = sign * (load * factors[member] + common_part) + 0.5 * noise
    values = jnp.clip(center + scale * signal, -32.0, 32.0)
    return values.astype(jnp.bfloat16)


def setup_inputs(seed: int = 0) -> dict:
    arg_keys = jax.random.split(jax.random.key(seed), 3)
    return {
        "expression": draw_expression(jax.random.fold_in(arg_keys[2], 71), 0),
        "panel_index": jax.random.randint(arg_keys[1], (1,), 0, GENES // PANEL).astype(jnp.int32),
    }


def standardize(expression):
    values = expression.astype(jnp.float32)
    center = values - lax.optimization_barrier(jnp.mean(values, axis=1, keepdims=True))
    spread = lax.optimization_barrier(jnp.mean(center * center, axis=1, keepdims=True))
    return (center * lax.rsqrt(spread + 1e-05)).astype(jnp.bfloat16)

def adjacency(left, right, left_gene, right_gene):
    corr = jnp.dot(left, right.T, preferred_element_type=jnp.float32) / SAMPLES
    square = corr * corr
    power = square * square * square
    return jnp.where(left_gene[:, None] == right_gene[None, :], jnp.zeros_like(power), power)

def reference(expression, panel_index):
    normed = standardize(expression)
    genes = jnp.arange(GENES, dtype=jnp.int32)
    first = (panel_index[0] * PANEL).astype(jnp.int32)
    panel_rows = lax.dynamic_slice_in_dim(normed, first, PANEL, 0)
    panel_genes = first + jnp.arange(PANEL, dtype=jnp.int32)
    panel_adj = adjacency(normed, panel_rows, genes, panel_genes)
    panel_deg = lax.optimization_barrier(jnp.sum(panel_adj, axis=0))
    panel_half = panel_adj.astype(jnp.bfloat16)
    height = min(1024, GENES)

    def one_block(index):
        start = (index * height).astype(jnp.int32)
        rows = lax.dynamic_slice_in_dim(normed, start, height, 0)
        row_genes = start + jnp.arange(height, dtype=jnp.int32)
        adj = adjacency(rows, normed, row_genes, genes)
        products = jnp.dot(adj.astype(jnp.bfloat16), panel_half, preferred_element_type=jnp.float32)
        return (lax.optimization_barrier(jnp.sum(adj, axis=1)), products)
    degree, shared = lax.map(one_block, jnp.arange(GENES // height, dtype=jnp.int32))
    degree = degree.reshape(GENES)
    shared = shared.reshape(GENES, PANEL)
    scaled_degree = degree / jnp.max(degree)
    lower = jnp.minimum(degree[:, None], panel_deg[None, :])
    correlation = (shared + panel_adj) / (lower + 1.0 - panel_adj)
    correlation = jnp.where(genes[:, None] == panel_genes[None, :], jnp.ones_like(correlation), correlation)
    return (scaled_degree, correlation)
```

```python
import itertools

import jax
import jax.numpy as jnp
import numpy as np
from jax import lax
from jax.experimental import pallas as pl
from jax.experimental.pallas import tpu as pltpu
from jax.sharding import Mesh
from jax.sharding import PartitionSpec as P

AXES = ("zl", "y", "core", "zh", "x")
SIZES = {"zl": 2, "y": 4, "core": 2, "zh": 4, "x": 4}
Z = ("zl", "zh")
ROWS_T = (((1,), (1,)), ((), ()))
F32 = jnp.float32
BF16 = jnp.bfloat16
VMEM = pl.BlockSpec(memory_space=pltpu.VMEM)
SMEM = pl.BlockSpec(memory_space=pltpu.SMEM)
MSG = 272


def pairs(axes, step):
    sizes = [SIZES[a] for a in axes]
    found = []
    for i, place in enumerate(itertools.product(*[range(s) for s in sizes])):
        at = dict(zip(axes, place))
        if axes == Z:
            at = {"z": at["zh"] * 2 + at["zl"]}
        src = step(at)
        if axes == Z:
            src = {"zl": src["z"] % 2, "zh": src["z"] // 2}
        found.append((int(np.ravel_multi_index([src[a] for a in axes], sizes)), i))
    return found


def recv(value, axis, delta):
    axes = Z if axis == "z" else (axis,)
    size = 8 if axis == "z" else SIZES[axis]
    return lax.ppermute(value, axes, pairs(axes, lambda at: {axis: (at[axis] + delta) % size}))


def swap(value, axis, mask):
    axes = Z if axis == "z" else (axis,)
    return lax.ppermute(value, axes, pairs(axes, lambda at: {axis: at[axis] ^ mask}))


def sixth(c):
    s = c * c
    return s * s * s


def standardize_kernel(x_ref, low_ref, high_ref):
    values = x_ref[...].astype(F32)
    center = values - jnp.mean(values, axis=1, keepdims=True)
    spread = jnp.mean(center * center, axis=1, keepdims=True)
    normed = (center * lax.rsqrt(spread + 1e-05)).astype(BF16) * BF16(0.0625)
    half = normed.shape[0] // 2
    low_ref[...] = normed[:half]
    high_ref[...] = normed[half:]


def standardize(x):
    shape = jax.ShapeDtypeStruct((x.shape[0] // 2, x.shape[1]), BF16)
    return pl.pallas_call(
        standardize_kernel, out_shape=[shape, shape], in_specs=[VMEM], out_specs=[VMEM, VMEM], name="standardize"
    )(x)


def split(v):
    hi = v.astype(BF16)
    return hi, (v - hi.astype(F32)).astype(BF16)


def tile_kernel(where_ref, own_ref, other_ref, zp_ref, *refs):
    cols = refs[:8]
    keep_ref, send_ref, pan, pdeg = refs[8:]
    zp = zp_ref[...]
    total = jnp.zeros((1, 128), F32)
    r = lax.broadcasted_iota(jnp.int32, (128, 128), 0)
    c = lax.broadcasted_iota(jnp.int32, (128, 128), 1)
    for b in range(8):
        for q in range(4):
            v = sixth(lax.dot_general(cols[b][q * 128 : (q + 1) * 128, :], zp, ROWS_T, preferred_element_type=F32))
            v = jnp.where((r == c) & (where_ref[0] == b * 4 + q), 0.0, v)
            total = total + jnp.sum(v, axis=0, keepdims=True)
            pan[pl.ds((b * 4 + q) * 128, 128), :128] = v.astype(BF16)
    pan[:, 128:] = jnp.ones((4096, 128), BF16)
    pdeg[...] = total

    def rows_tile(rows, own):
        acc = None
        height = rows.shape[0]
        for j in range(16):
            zc = cols[j // 2][(j % 2) * 256 : (j % 2) * 256 + 256, :]
            a = sixth(lax.dot_general(rows, zc, ROWS_T, preferred_element_type=F32))
            if own is not None and j in (0, 8):
                gene = lax.broadcasted_iota(jnp.int32, (height, 256), 0) + own
                col = lax.broadcasted_iota(jnp.int32, (height, 256), 1)
                same = (gene == col) & (col < 128) if j == 0 else (gene == col + 128) & (col < 128)
                a = jnp.where(same, 0.0, a)
            d = jnp.dot(a.astype(BF16), pan[pl.ds(j * 256, 256), :], preferred_element_type=F32)
            acc = d if acc is None else acc + d
        return acc

    def degree_rows(acc, k):
        flat = acc[k * 256 : (k + 1) * 256, 128:]
        return flat[:128].T[0:1], flat[128:].T[0:1]

    def own_step(i, carry):
        acc = rows_tile(own_ref[pl.ds(i * 1024, 1024), :], i * 1024)
        for k in range(4):
            keep_ref[i * 4 + k, :256, :] = acc[k * 256 : (k + 1) * 256, :128]
            d0, d1 = degree_rows(acc, k)
            keep_ref[i * 4 + k, 256:, :] = jnp.concatenate([d0, d1, pdeg[...], jnp.zeros((13, 128), F32)], axis=0)
        return carry

    def other_step(i, carry):
        acc = rows_tile(other_ref[pl.ds(i * 1024, 1024), :], None)
        for k in range(4):
            send_ref[i * 4 + k, :256, :] = acc[k * 256 : (k + 1) * 256, :128].astype(BF16)
            d0, d1 = degree_rows(acc, k)
            tail = jnp.concatenate([d0, d1, pdeg[...], jnp.zeros((5, 128), F32)], axis=0)
            hi = tail.astype(BF16).astype(F32)
            send_ref[i * 4 + k, 256:, :] = jnp.concatenate([hi, tail - hi], axis=0).astype(BF16)
        return carry

    lax.fori_loop(0, 2, other_step, 0)
    lax.fori_loop(0, 2, own_step, 0)


def tile(where, own, other, zp, cols):
    return pl.pallas_call(
        tile_kernel,
        out_shape=[jax.ShapeDtypeStruct((8, MSG, 128), F32), jax.ShapeDtypeStruct((8, MSG, 128), BF16)],
        in_specs=[SMEM] + [VMEM] * 11,
        out_specs=[VMEM, VMEM],
        scratch_shapes=[pltpu.VMEM((4096, 256), BF16), pltpu.VMEM((1, 128), F32)],
        compiler_params=pltpu.CompilerParams(vmem_limit_bytes=48 * 2**20),
        cost_estimate=pl.CostEstimate(flops=18 * 10**9, bytes_accessed=10**7, transcendentals=0),
        name="tile",
    )(where, own, other, zp, *cols)


def unpack(msg):
    return msg[:256].astype(F32), msg[256:264].astype(F32) + msg[264:272].astype(F32)


def combine_kernel(keep_ref, got_ref, sum_ref, send_ref):
    for k in range(8):
        p, t = unpack(got_ref[k])
        p = p + keep_ref[k, :256, :]
        t = t + keep_ref[k, 256:264, :]
        if k == 0:
            sum_ref[:256, :] = p
            sum_ref[256:, :] = t
        else:
            send_ref[k - 1, :256, :] = p.astype(BF16)
            hi = t.astype(BF16).astype(F32)
            send_ref[k - 1, 256:, :] = jnp.concatenate([hi, t - hi], axis=0).astype(BF16)


def combine(keep, got):
    return pl.pallas_call(
        combine_kernel,
        out_shape=[jax.ShapeDtypeStruct((264, 128), F32), jax.ShapeDtypeStruct((7, MSG, 128), BF16)],
        in_specs=[VMEM, VMEM],
        out_specs=[VMEM, VMEM],
        name="combine",
    )(keep, got)


def finish_kernel(sum_ref, *refs):
    gots, (total_ref, top_ref) = refs[:7], refs[7:]
    p, t = sum_ref[:256, :], sum_ref[256:, :]
    for g in gots:
        dp, dt = unpack(g[...])
        p, t = p + dp, t + dt
    total_ref[:256, :] = p
    total_ref[256:, :] = t
    top_ref[...] = jnp.broadcast_to(jnp.max(t[0:2], keepdims=True), (8, 128))


def finish(own, gots):
    return pl.pallas_call(
        finish_kernel,
        out_shape=[jax.ShapeDtypeStruct((264, 128), F32), jax.ShapeDtypeStruct((8, 128), F32)],
        in_specs=[VMEM] * 8,
        out_specs=[VMEM, VMEM],
        name="finish",
    )(own, *gots)


def correlation_kernel(where_ref, total_ref, low_ref, high_ref, zp_ref, out_ref):
    zp = zp_ref[...]
    r = lax.broadcasted_iota(jnp.int32, (128, 128), 0)
    c = lax.broadcasted_iota(jnp.int32, (128, 128), 1)
    for half, ref in enumerate((low_ref, high_ref)):
        direct = sixth(lax.dot_general(ref[...], zp, ROWS_T, preferred_element_type=F32))
        same = (r == c) & (where_ref[0] == half * 16)
        direct = jnp.where(same, 0.0, direct)
        degree = jnp.broadcast_to(total_ref[256 + half : 257 + half, :], (128, 128)).T
        lower = jnp.minimum(degree, total_ref[258:259, :])
        value = (total_ref[half * 128 : half * 128 + 128, :] + direct) / (lower + 1.0 - direct)
        out_ref[half * 128 : half * 128 + 128, :] = jnp.where(same, 1.0, value)


def correlate(where, total, low, high, zp):
    return pl.pallas_call(
        correlation_kernel,
        out_shape=jax.ShapeDtypeStruct((256, 128), F32),
        in_specs=[SMEM] + [VMEM] * 4,
        out_specs=VMEM,
        name="correlate",
    )(where, total, low, high, zp)


def pick(parts, index):
    out = parts[0]
    for k in range(1, len(parts)):
        out = jnp.where(index == k, parts[k], out)
    return out


def on_device(expression, panel_index):
    at = {a: lax.axis_index(a) for a in AXES}
    z = at["zh"] * 2 + at["zl"]
    low, high = standardize(expression)

    start = panel_index[0]
    half = start % 2
    holder = start // 2
    hx = holder % 4
    hz = (holder // 4) % 4 * 2 + holder // 128
    hk = holder // 16 % 2
    hy = holder // 32 % 4
    dx, dy, dz = (hx - at["x"]) % 4, (hy - at["y"]) % 4, (hz - z) % 8
    same_line = (dz == 0) & (hk == at["core"])
    piece = jnp.where(half == 0, dy * 4 + dx, 16 + dx * 4 + dy)
    where = jnp.where(same_line, piece, -1).astype(jnp.int32)[None]

    block = jnp.concatenate([low, high])
    line = [block] + [recv(block, "z", d) for d in range(1, 8)]
    own = jnp.concatenate(line)
    other = swap(own, "core", 1)

    part = lax.dynamic_slice_in_dim(own, dz * 256 + half * 128, 128, 0)
    part = pick([part, swap(part, "core", 1)], hk ^ at["core"])
    part = pick([part] + [recv(part, "y", d) for d in range(1, 4)], dy)
    zp = pick([part] + [recv(part, "x", d) for d in range(1, 4)], dx)

    low_x = jnp.concatenate([low] + [recv(low, "x", d) for d in range(1, 4)])
    high_y = jnp.concatenate([high] + [recv(high, "y", d) for d in range(1, 4)])
    low_xy = [low_x] + [recv(low_x, "y", d) for d in range(1, 4)]
    high_yx = [high_y] + [recv(high_y, "x", d) for d in range(1, 4)]

    keep, send = tile(where, own, other, zp, low_xy + high_yx)
    got = swap(send, "core", 1)
    mine, sends = combine(keep, got)
    gots = [recv(sends[8 - d - 1], "z", d) for d in range(1, 8)]
    total, top = finish(mine, gots)
    for axis, mask in (("core", 1), ("x", 1), ("x", 3), ("y", 1), ("y", 3), ("z", 1), ("z", 3), ("z", 7)):
        top = jnp.maximum(top, swap(top, axis, mask))
    correlation = correlate(where, total, low, high, zp)
    scaled_degree = total[256:258].reshape(256) / top[0, 0]
    return (scaled_degree, correlation)


def solution(mesh):
    inner = Mesh(mesh.devices.reshape([SIZES[a] for a in AXES]), AXES)
    return jax.shard_map(
        on_device,
        mesh=inner,
        in_specs=(P(AXES, None), P()),
        out_specs=(P(AXES), P(AXES, None)),
        check_vma=False,
    )
```

```python
import jax
import jax.numpy as jnp
from jax import lax
from jax.experimental import pallas as pl
from jax.experimental.pallas import tpu as pltpu
from jax.sharding import Mesh
from jax.sharding import PartitionSpec as P

AXES = ("zl", "y", "core", "zh", "x")
SIZES = {"zl": 2, "y": 4, "core": 2, "zh": 4, "x": 4}
ROWS_T = (((1,), (1,)), ((), ()))
F32 = jnp.float32
BF16 = jnp.bfloat16
VMEM = pl.BlockSpec(memory_space=pltpu.VMEM)
SMEM = pl.BlockSpec(memory_space=pltpu.SMEM)
MSG = 272
LAST = 288


def recv(value, axis, delta):
    size = SIZES[axis]
    return lax.ppermute(value, axis, [((i + delta) % size, i) for i in range(size)])


def ring(value, axis):
    return [value] + [recv(value, axis, d) for d in range(1, SIZES[axis])]


def after(value, *others):
    return lax.optimization_barrier((value, *others))[0]


def sixth(c):
    s = c * c
    return s * s * s


def split_rows(v):
    hi = v.astype(BF16).astype(F32)
    return jnp.concatenate([hi, v - hi], axis=0).astype(BF16)


def standardize_kernel(x_ref, out_ref):
    values = x_ref[...].astype(F32)
    center = values - jnp.mean(values, axis=1, keepdims=True)
    spread = jnp.mean(center * center, axis=1, keepdims=True)
    out_ref[...] = (center * lax.rsqrt(spread + 1e-05)).astype(BF16) * BF16(0.0625)


def standardize(x):
    return pl.pallas_call(
        standardize_kernel,
        out_shape=jax.ShapeDtypeStruct(x.shape, BF16),
        in_specs=[VMEM],
        out_specs=VMEM,
        name="standardize",
    )(x)


def panel_kernel(where_ref, c0_ref, c1_ref, zp_ref, pan_ref, pdeg_ref):
    zp = zp_ref[...]
    total = jnp.zeros((1, 128), F32)
    r = lax.broadcasted_iota(jnp.int32, (128, 128), 0)
    c = lax.broadcasted_iota(jnp.int32, (128, 128), 1)
    for g in range(32):
        ref = (c0_ref, c1_ref)[g // 16]
        rows = ref[(g % 16) * 128 : (g % 16) * 128 + 128, :]
        v = sixth(lax.dot_general(rows, zp, ROWS_T, preferred_element_type=F32))
        v = jnp.where((r == c) & (where_ref[0] == g), 0.0, v)
        total = total + jnp.sum(v, axis=0, keepdims=True)
        pan_ref[g * 128 : g * 128 + 128, :128] = v.astype(BF16)
    pan_ref[:, 128:] = jnp.ones((4096, 128), BF16)
    pdeg_ref[...] = jnp.broadcast_to(total, (8, 128))


def panel_matrix(where, cols, zp):
    return pl.pallas_call(
        panel_kernel,
        out_shape=[jax.ShapeDtypeStruct((4096, 256), BF16), jax.ShapeDtypeStruct((8, 128), F32)],
        in_specs=[SMEM] + [VMEM] * 3,
        out_specs=[VMEM, VMEM],
        cost_estimate=pl.CostEstimate(flops=10**9, bytes_accessed=10**6, transcendentals=0),
        name="panel_matrix",
    )(where, *cols, zp)


def chunk_sums(rows_ref, c0_ref, c1_ref, pan_ref, own):
    acc = None
    rows = rows_ref[...]
    for j in range(16):
        zc = (c0_ref, c1_ref)[j // 8][(j % 8) * 256 : (j % 8) * 256 + 256, :]
        a = sixth(lax.dot_general(rows, zc, ROWS_T, preferred_element_type=F32))
        if own and j == 0:
            gene = lax.broadcasted_iota(jnp.int32, a.shape, 0)
            a = jnp.where(gene == lax.broadcasted_iota(jnp.int32, a.shape, 1), 0.0, a)
        d = jnp.dot(a.astype(BF16), pan_ref[j * 256 : j * 256 + 256, :], preferred_element_type=F32)
        acc = d if acc is None else acc + d
    return acc


def degree_rows(acc, k):
    flat = acc[k * 256 : k * 256 + 256, 128:]
    return [flat[:128].T[0:1], flat[128:].T[0:1]]


def away_kernel(rows_ref, c0_ref, c1_ref, pan_ref, pdeg_ref, send_ref):
    acc = chunk_sums(rows_ref, c0_ref, c1_ref, pan_ref, False)
    for k in range(4):
        send_ref[k, :256, :] = acc[k * 256 : k * 256 + 256, :128].astype(BF16)
        tail = jnp.concatenate(degree_rows(acc, k) + [pdeg_ref[0:1, :], jnp.zeros((5, 128), F32)], axis=0)
        send_ref[k, 256:, :] = split_rows(tail)


CHUNK = dict(
    compiler_params=pltpu.CompilerParams(vmem_limit_bytes=32 * 2**20),
    cost_estimate=pl.CostEstimate(flops=45 * 10**8, bytes_accessed=4 * 10**6, transcendentals=0),
)


def away(rows, cols, pan, pdeg):
    return pl.pallas_call(
        away_kernel,
        out_shape=jax.ShapeDtypeStruct((4, MSG, 128), BF16),
        in_specs=[VMEM] * 5,
        out_specs=VMEM,
        name="tile_away",
        **CHUNK,
    )(rows, *cols, pan, pdeg)


def home_kernel(rows_ref, c0_ref, c1_ref, pan_ref, pdeg_ref, g0, g1, g2, sum_ref, send_ref):
    acc = chunk_sums(rows_ref, c0_ref, c1_ref, pan_ref, True)
    products, degrees = [], []
    pdeg = pdeg_ref[0:1, :]
    for k in range(4):
        p = acc[k * 256 : k * 256 + 256, :128]
        d = jnp.concatenate(degree_rows(acc, k), axis=0)
        for g in (g0, g1, g2):
            p = p + g[k, :256, :].astype(F32)
            t = g[k, 256:264, :].astype(F32) + g[k, 264:272, :].astype(F32)
            d = d + t[0:2]
            if k == 0:
                pdeg = pdeg + t[2:3]
        products.append(p)
        degrees.append(d)
    for k in range(4):
        turned = [degrees[(k + i) % 4] for i in range(4)]
        tail = jnp.concatenate(turned + [pdeg, jnp.zeros((7, 128), F32)], axis=0)
        if k == 0:
            sum_ref[:256, :] = products[0]
            sum_ref[256:, :] = tail
        else:
            send_ref[k - 1, :256, :] = products[k].astype(BF16)
            send_ref[k - 1, 256:, :] = split_rows(tail)


def home(rows, cols, pan, pdeg, gots):
    return pl.pallas_call(
        home_kernel,
        out_shape=[jax.ShapeDtypeStruct((272, 128), F32), jax.ShapeDtypeStruct((3, LAST, 128), BF16)],
        in_specs=[VMEM] * 8,
        out_specs=[VMEM, VMEM],
        name="tile_home",
        **CHUNK,
    )(rows, *cols, pan, pdeg, *gots)


def finish_kernel(sum_ref, g0, g1, g2, total_ref, top_ref):
    p, t = sum_ref[:256, :], sum_ref[256:, :]
    for g in (g0, g1, g2):
        p = p + g[:256, :].astype(F32)
        t = t + (g[256:272, :].astype(F32) + g[272:288, :].astype(F32))
    total_ref[:256, :] = p
    total_ref[256:, :] = t
    top_ref[...] = jnp.broadcast_to(jnp.max(t[0:8], keepdims=True), (8, 128))


def finish(own, gots):
    return pl.pallas_call(
        finish_kernel,
        out_shape=[jax.ShapeDtypeStruct((272, 128), F32), jax.ShapeDtypeStruct((8, 128), F32)],
        in_specs=[VMEM] * 4,
        out_specs=[VMEM, VMEM],
        name="finish",
    )(own, *gots)


def correlation_kernel(where_ref, total_ref, block_ref, zp_ref, out_ref):
    zp = zp_ref[...]
    r = lax.broadcasted_iota(jnp.int32, (128, 128), 0)
    c = lax.broadcasted_iota(jnp.int32, (128, 128), 1)
    for half in range(2):
        rows = slice(half * 128, half * 128 + 128)
        direct = sixth(lax.dot_general(block_ref[rows, :], zp, ROWS_T, preferred_element_type=F32))
        same = (r == c) & (where_ref[0] == half)
        direct = jnp.where(same, 0.0, direct)
        degree = jnp.broadcast_to(total_ref[256 + half : 257 + half, :], (128, 128)).T
        lower = jnp.minimum(degree, total_ref[264:265, :])
        value = (total_ref[rows, :] + direct) / (lower + 1.0 - direct)
        out_ref[rows, :] = jnp.where(same, 1.0, value)


def correlate(where, total, block, zp):
    return pl.pallas_call(
        correlation_kernel,
        out_shape=jax.ShapeDtypeStruct((256, 128), F32),
        in_specs=[SMEM] + [VMEM] * 3,
        out_specs=VMEM,
        name="correlate",
    )(where, total, block, zp)


def scale_kernel(total_ref, t0, t1, t2, t3, out_ref):
    top = jnp.maximum(jnp.maximum(t0[...], t1[...]), jnp.maximum(t2[...], t3[...]))
    out_ref[...] = total_ref[256:258, :] / top[0:2, :]


def scale(total, tops):
    return pl.pallas_call(
        scale_kernel,
        out_shape=jax.ShapeDtypeStruct((2, 128), F32),
        in_specs=[VMEM] * 5,
        out_specs=VMEM,
        name="scale",
    )(total, *tops)


def pick(parts, index):
    out = parts[0]
    for k in range(1, len(parts)):
        out = jnp.where(index == k, parts[k], out)
    return out


def highest(parts):
    out = parts[0]
    for part in parts[1:]:
        out = jnp.maximum(out, part)
    return out


def on_device(expression, panel_index):
    at = {a: lax.axis_index(a) for a in AXES}
    block = standardize(expression)

    half = panel_index[0] % 2
    rest = panel_index[0] // 2
    far = {}
    for a in reversed(AXES):
        far[a] = (rest % SIZES[a] - at[a]) % SIZES[a]
        rest = rest // SIZES[a]
    place = far["y"] * 4 + far["zl"] * 2 + half
    here = (far["x"] == 0) & (far["zh"] == 0)
    where = jnp.where(here, far["core"] * 16 + place, -1).astype(jnp.int32)[None]

    pair = jnp.concatenate(ring(block, "zl"))
    near = jnp.concatenate(ring(pair, "y"))
    cols = (near, recv(near, "core", 1))

    group = jnp.concatenate(ring(block, "zh"))
    rows = ring(group, "x")

    zp = lax.dynamic_slice_in_dim(near, place * 128, 128, 0)
    for a in ("core", "zh", "x"):
        zp = pick(ring(zp, a), far[a])

    pan, pdeg = panel_matrix(where, cols, zp)
    gots = []
    for d in (2, 1, 3):
        gots.append(recv(away(rows[d], cols, pan, pdeg), "x", 4 - d))
    mine, sends = home(rows[0], cols, pan, pdeg, gots)
    total, top = finish(mine, [recv(sends[k - 1], "zh", 4 - k) for k in (1, 2, 3)])
    for a in ("core", "zl", "x"):
        top = highest(ring(top, a))
    correlation = correlate(where, total, block, zp)
    return (scale(total, ring(top, "y")).reshape(256), correlation)


def solution(mesh):
    inner = Mesh(mesh.devices.reshape([SIZES[a] for a in AXES]), AXES)
    return jax.shard_map(
        on_device,
        mesh=inner,
        in_specs=(P(AXES, None), P()),
        out_specs=(P(AXES), P(AXES, None)),
        check_vma=False,
    )
```

```python
import jax
import jax.numpy as jnp
from jax import lax
from jax.experimental import pallas as pl
from jax.experimental.pallas import tpu as pltpu
from jax.sharding import Mesh
from jax.sharding import PartitionSpec as P

AXES = ("zl", "y", "core", "zh", "x")
SIZES = {"zl": 2, "y": 4, "core": 2, "zh": 4, "x": 4}
ROWS_T = (((1,), (1,)), ((), ()))
F32 = jnp.float32
BF16 = jnp.bfloat16
VMEM = pl.BlockSpec(memory_space=pltpu.VMEM)
SMEM = pl.BlockSpec(memory_space=pltpu.SMEM)
MSG = 272
LAST = 288
PEER_AXES = ("zl", "y", "core", "x")
PEERS = 64


def recv(value, axis, delta):
    size = SIZES[axis]
    return lax.ppermute(value, axis, [((i + delta) % size, i) for i in range(size)])


def ring(value, axis):
    return [value] + [recv(value, axis, d) for d in range(1, SIZES[axis])]


def after(value, *others):
    return lax.optimization_barrier((value, *others))[0]


def sixth(c):
    s = c * c
    return s * s * s


def split_rows(v):
    hi = v.astype(BF16).astype(F32)
    return jnp.concatenate([hi, v - hi], axis=0).astype(BF16)


def standardize_kernel(x_ref, out_ref):
    values = x_ref[...].astype(F32)
    center = values - jnp.mean(values, axis=1, keepdims=True)
    spread = jnp.mean(center * center, axis=1, keepdims=True)
    out_ref[...] = (center * lax.rsqrt(spread + 1e-05)).astype(BF16) * BF16(0.0625)


def standardize(x):
    return pl.pallas_call(
        standardize_kernel,
        out_shape=jax.ShapeDtypeStruct(x.shape, BF16),
        in_specs=[VMEM],
        out_specs=VMEM,
        name="standardize",
    )(x)


def panel_kernel(where_ref, c0_ref, c1_ref, zp_ref, pan_ref, pdeg_ref):
    zp = zp_ref[...]
    total = jnp.zeros((1, 128), F32)
    r = lax.broadcasted_iota(jnp.int32, (512, 128), 0)
    c = lax.broadcasted_iota(jnp.int32, (512, 128), 1)
    for g in range(8):
        rows = (c0_ref, c1_ref)[g // 4][(g % 4) * 512 : (g % 4) * 512 + 512, :]
        v = sixth(lax.dot_general(rows, zp, ROWS_T, preferred_element_type=F32))
        v = jnp.where(r + g * 512 == c + where_ref[0] * 128, 0.0, v)
        total = total + jnp.sum(v, axis=0, keepdims=True)
        pan_ref[g * 512 : g * 512 + 512, :128] = v.astype(BF16)
    pan_ref[:, 128:] = jnp.ones((4096, 128), BF16)
    pdeg_ref[...] = jnp.broadcast_to(total, (8, 128))


def chunk_sums(rows_ref, c0_ref, c1_ref, pan_ref, own):
    acc = None
    rows = rows_ref[...]
    for j in range(16):
        zc = (c0_ref, c1_ref)[j // 8][(j % 8) * 256 : (j % 8) * 256 + 256, :]
        a = sixth(lax.dot_general(rows, zc, ROWS_T, preferred_element_type=F32))
        if own and j == 0:
            gene = lax.broadcasted_iota(jnp.int32, a.shape, 0)
            a = jnp.where(gene == lax.broadcasted_iota(jnp.int32, a.shape, 1), 0.0, a)
        d = jnp.dot(a.astype(BF16), pan_ref[j * 256 : j * 256 + 256, :], preferred_element_type=F32)
        acc = d if acc is None else acc + d
    return acc


def degree_rows(acc, k):
    flat = acc[k * 256 : k * 256 + 256, 128:]
    return [flat[:128].T[0:1], flat[128:].T[0:1]]


def away_kernel(rows_ref, c0_ref, c1_ref, pan_ref, pdeg_ref, send_ref):
    acc = chunk_sums(rows_ref, c0_ref, c1_ref, pan_ref, False)
    for k in range(4):
        send_ref[k, :256, :] = acc[k * 256 : k * 256 + 256, :128].astype(BF16)
        tail = jnp.concatenate(degree_rows(acc, k) + [pdeg_ref[0:1, :], jnp.zeros((5, 128), F32)], axis=0)
        send_ref[k, 256:, :] = split_rows(tail)


CHUNK = dict(
    compiler_params=pltpu.CompilerParams(vmem_limit_bytes=16 * 2**20),
    cost_estimate=pl.CostEstimate(flops=45 * 10**8, bytes_accessed=4 * 10**6, transcendentals=0),
)


def away(rows, cols, pan, pdeg):
    return pl.pallas_call(
        away_kernel,
        out_shape=jax.ShapeDtypeStruct((4, MSG, 128), BF16),
        in_specs=[VMEM] * 5,
        out_specs=VMEM,
        name="tile_away",
        **CHUNK,
    )(rows, *cols, pan, pdeg)


def first_kernel(where_ref, rows_ref, c0_ref, c1_ref, zp_ref, pan_ref, pdeg_ref, send_ref):
    panel_kernel(where_ref, c0_ref, c1_ref, zp_ref, pan_ref, pdeg_ref)
    away_kernel(rows_ref, c0_ref, c1_ref, pan_ref, pdeg_ref, send_ref)


def first(where, rows, cols, zp):
    return pl.pallas_call(
        first_kernel,
        out_shape=[
            jax.ShapeDtypeStruct((4096, 256), BF16),
            jax.ShapeDtypeStruct((8, 128), F32),
            jax.ShapeDtypeStruct((4, MSG, 128), BF16),
        ],
        in_specs=[SMEM] + [VMEM] * 4,
        out_specs=[VMEM] * 3,
        name="tile_first",
        **CHUNK,
    )(where, rows, *cols, zp)


def home_kernel(rows_ref, c0_ref, c1_ref, pan_ref, sum_ref, deg_ref):
    acc = chunk_sums(rows_ref, c0_ref, c1_ref, pan_ref, True)
    sum_ref[...] = acc[:, :128]
    deg_ref[...] = jnp.concatenate(sum([degree_rows(acc, k) for k in range(4)], []), axis=0)


def home(rows, cols, pan):
    return pl.pallas_call(
        home_kernel,
        out_shape=[jax.ShapeDtypeStruct((1024, 128), F32), jax.ShapeDtypeStruct((8, 128), F32)],
        in_specs=[VMEM] * 4,
        out_specs=[VMEM, VMEM],
        name="tile_home",
        **CHUNK,
    )(rows, *cols, pan)


def combine_kernel(home_ref, deg_ref, pdeg_ref, g0, g1, g2, sum_ref, *sends):
    degrees = []
    pdeg = pdeg_ref[0:1, :]
    for k in range(4):
        p = home_ref[k * 256 : k * 256 + 256, :]
        d = deg_ref[k * 2 : k * 2 + 2, :]
        for g in (g0, g1, g2):
            p = p + g[k, :256, :].astype(F32)
            t = g[k, 256:264, :].astype(F32) + g[k, 264:272, :].astype(F32)
            d = d + t[0:2]
            if k == 0:
                pdeg = pdeg + t[2:3]
        if k == 0:
            sum_ref[:256, :] = p
        else:
            sends[k - 1][:256, :] = p.astype(BF16)
        degrees.append(d)
    for k in range(4):
        turned = [degrees[(k + i) % 4] for i in range(4)]
        tail = jnp.concatenate(turned + [pdeg, jnp.zeros((7, 128), F32)], axis=0)
        if k == 0:
            sum_ref[256:, :] = tail
        else:
            sends[k - 1][256:, :] = split_rows(tail)


def combine(products, degrees, pdeg, gots):
    return pl.pallas_call(
        combine_kernel,
        out_shape=[jax.ShapeDtypeStruct((272, 128), F32)] + [jax.ShapeDtypeStruct((LAST, 128), BF16)] * 3,
        in_specs=[VMEM] * 6,
        out_specs=[VMEM] * 4,
        name="combine",
    )(products, degrees, pdeg, *gots)


def finish_kernel(sum_ref, g0, g1, g2, total_ref, top_ref):
    p, t = sum_ref[:256, :], sum_ref[256:, :]
    for g in (g0, g1, g2):
        p = p + g[:256, :].astype(F32)
        t = t + (g[256:272, :].astype(F32) + g[272:288, :].astype(F32))
    total_ref[:256, :] = p
    total_ref[256:, :] = t
    top_ref[...] = jnp.broadcast_to(jnp.max(t[0:8], keepdims=True)[None], top_ref.shape)


def finish(own, gots):
    return pl.pallas_call(
        finish_kernel,
        out_shape=[jax.ShapeDtypeStruct((272, 128), F32), jax.ShapeDtypeStruct((PEERS, 8, 128), F32)],
        in_specs=[VMEM] * 4,
        out_specs=[VMEM, VMEM],
        name="finish",
    )(own, *gots)


def correlation_kernel(where_ref, total_ref, block_ref, zp_ref, out_ref):
    zp = zp_ref[...]
    r = lax.broadcasted_iota(jnp.int32, (128, 128), 0)
    c = lax.broadcasted_iota(jnp.int32, (128, 128), 1)
    for half in range(2):
        rows = slice(half * 128, half * 128 + 128)
        direct = sixth(lax.dot_general(block_ref[rows, :], zp, ROWS_T, preferred_element_type=F32))
        same = (r == c) & (where_ref[0] == half)
        direct = jnp.where(same, 0.0, direct)
        degree = jnp.broadcast_to(total_ref[256 + half : 257 + half, :], (128, 128)).T
        lower = jnp.minimum(degree, total_ref[264:265, :])
        value = (total_ref[rows, :] + direct) / (lower + 1.0 - direct)
        out_ref[rows, :] = jnp.where(same, 1.0, value)


def correlate(where, total, block, zp):
    return pl.pallas_call(
        correlation_kernel,
        out_shape=jax.ShapeDtypeStruct((256, 128), F32),
        in_specs=[SMEM] + [VMEM] * 3,
        out_specs=VMEM,
        name="correlate",
    )(where, total, block, zp)


def scale_kernel(total_ref, tops_ref, out_ref):
    out_ref[...] = total_ref[256:258, :] / jnp.max(tops_ref[...], axis=0)[0:2]


def scale(total, tops):
    return pl.pallas_call(
        scale_kernel,
        out_shape=jax.ShapeDtypeStruct((2, 128), F32),
        in_specs=[VMEM] * 2,
        out_specs=VMEM,
        name="scale",
    )(total, tops)


def pick(parts, index):
    out = parts[0]
    for k in range(1, len(parts)):
        out = jnp.where(index == k, parts[k], out)
    return out


def on_device(expression, panel_index):
    at = {a: lax.axis_index(a) for a in AXES}
    block = standardize(expression)

    half = panel_index[0] % 2
    rest = panel_index[0] // 2
    far = {}
    for a in reversed(AXES):
        far[a] = (rest % SIZES[a] - at[a]) % SIZES[a]
        rest = rest // SIZES[a]
    place = far["y"] * 4 + far["zl"] * 2 + half
    here = (far["x"] == 0) & (far["zh"] == 0)
    where = jnp.where(here, far["core"] * 16 + place, -1).astype(jnp.int32)[None]

    group = jnp.concatenate(ring(block, "zh"))
    pair = jnp.concatenate(ring(block, "zl"))
    group, pair = lax.optimization_barrier((group, pair))

    def panel_part(rows):
        return lax.dynamic_slice_in_dim(rows, far["zh"] * 256 + half * 128, 128, 0)

    zp = panel_part(group)
    opposite = recv(zp, "x", 2)
    near = jnp.concatenate(ring(pair, "y"))
    right, left = recv(group, "x", 1), recv(group, "x", 3)
    opposite, near, right, left = lax.optimization_barrier((opposite, near, right, left))

    zp = pick([zp, panel_part(right), opposite, panel_part(left)], far["x"])
    zp = pick(ring(zp, "zl"), far["zl"])
    apart = recv(right[:512], "x", 1), recv(left[512:], "x", 3)
    cols = (near, recv(near, "core", 1))
    zp = pick(ring(zp, "y"), far["y"])
    zp = pick(ring(zp, "core"), far["core"])

    pan, pdeg, part = first(where, right, cols, zp)
    gots = [recv(part, "x", 3)]
    near_half, far_half, part = lax.optimization_barrier((*apart, part))
    part = away(jnp.concatenate([near_half, far_half]), cols, pan, pdeg)
    gots.append(recv(part, "x", 2))
    part = away(after(left, part, gots[0]), cols, pan, pdeg)
    gots.append(recv(part, "x", 1))
    own, degrees = home(after(group, part), cols, pan)
    mine, *sends = combine(own, degrees, pdeg, gots)
    total, top = finish(mine, [recv(sends[k - 1], "zh", 4 - k) for k in (1, 2, 3)])
    tops = lax.all_to_all(top, PEER_AXES, 0, 0)
    correlation = correlate(where, total, block, zp)
    return (scale(total, tops).reshape(256), correlation)


def solution(mesh):
    inner = Mesh(mesh.devices.reshape([SIZES[a] for a in AXES]), AXES)
    return jax.shard_map(
        on_device,
        mesh=inner,
        in_specs=(P(AXES, None), P()),
        out_specs=(P(AXES), P(AXES, None)),
        check_vma=False,
    )
```

```python
import jax
import jax.numpy as jnp
from jax import lax
from jax.experimental import pallas as pl
from jax.experimental.pallas import tpu as pltpu
from jax.sharding import Mesh
from jax.sharding import PartitionSpec as P

AXES = ("zl", "y", "core", "zh", "x")
SIZES = {"zl": 2, "y": 4, "core": 2, "zh": 4, "x": 4}
ROWS_T = (((1,), (1,)), ((), ()))
F32 = jnp.float32
BF16 = jnp.bfloat16
VMEM = pl.BlockSpec(memory_space=pltpu.VMEM)
SMEM = pl.BlockSpec(memory_space=pltpu.SMEM)
MSG = 272
LAST = 288
PEER_AXES = ("zl", "y", "core", "x")
PEERS = 64


def recv(value, axis, delta):
    size = SIZES[axis]
    return lax.ppermute(value, axis, [((i + delta) % size, i) for i in range(size)])


def ring(value, axis):
    return [value] + [recv(value, axis, d) for d in range(1, SIZES[axis])]


def after(value, *others):
    return lax.optimization_barrier((value, *others))[0]


def sixth(c):
    s = c * c
    return s * s * s


def split_rows(v):
    hi = v.astype(BF16).astype(F32)
    return jnp.concatenate([hi, v - hi], axis=0).astype(BF16)


def standardize_kernel(x_ref, out_ref):
    values = x_ref[...].astype(F32)
    center = values - jnp.mean(values, axis=1, keepdims=True)
    spread = jnp.mean(center * center, axis=1, keepdims=True)
    out_ref[...] = (center * lax.rsqrt(spread + 1e-05)).astype(BF16) * BF16(0.0625)


def standardize(x):
    return pl.pallas_call(
        standardize_kernel,
        out_shape=jax.ShapeDtypeStruct(x.shape, BF16),
        in_specs=[VMEM],
        out_specs=VMEM,
        name="standardize",
        compiler_params=SMALL,
    )(x)


def panel_kernel(where_ref, c0_ref, c1_ref, zp_ref, pan_ref, pdeg_ref):
    zp = zp_ref[...]
    total = jnp.zeros((1, 128), F32)
    r = lax.broadcasted_iota(jnp.int32, (512, 128), 0)
    c = lax.broadcasted_iota(jnp.int32, (512, 128), 1)
    for g in range(8):
        rows = (c0_ref, c1_ref)[g // 4][(g % 4) * 512 : (g % 4) * 512 + 512, :]
        v = sixth(lax.dot_general(rows, zp, ROWS_T, preferred_element_type=F32))
        v = jnp.where(r + g * 512 == c + where_ref[0] * 128, 0.0, v)
        total = total + jnp.sum(v, axis=0, keepdims=True)
        pan_ref[g * 512 : g * 512 + 512, :128] = v.astype(BF16)
    pan_ref[:, 128:] = jnp.ones((4096, 128), BF16)
    pdeg_ref[...] = jnp.broadcast_to(total, (8, 128))


def chunk_sums(rows_ref, c0_ref, c1_ref, pan_ref, own):
    acc = None
    rows = rows_ref[...]
    for j in range(16):
        zc = (c0_ref, c1_ref)[j // 8][(j % 8) * 256 : (j % 8) * 256 + 256, :]
        a = sixth(lax.dot_general(rows, zc, ROWS_T, preferred_element_type=F32))
        if own and j == 0:
            gene = lax.broadcasted_iota(jnp.int32, a.shape, 0)
            a = jnp.where(gene == lax.broadcasted_iota(jnp.int32, a.shape, 1), 0.0, a)
        d = jnp.dot(a.astype(BF16), pan_ref[j * 256 : j * 256 + 256, :], preferred_element_type=F32)
        acc = d if acc is None else acc + d
    return acc


def degree_rows(acc, k):
    flat = acc[k * 256 : k * 256 + 256, 128:]
    return [flat[:128].T[0:1], flat[128:].T[0:1]]


def away_kernel(rows_ref, c0_ref, c1_ref, pan_ref, pdeg_ref, send_ref):
    acc = chunk_sums(rows_ref, c0_ref, c1_ref, pan_ref, False)
    for k in range(4):
        send_ref[k, :256, :] = acc[k * 256 : k * 256 + 256, :128].astype(BF16)
        tail = jnp.concatenate(degree_rows(acc, k) + [pdeg_ref[0:1, :], jnp.zeros((5, 128), F32)], axis=0)
        send_ref[k, 256:, :] = split_rows(tail)


SMALL = pltpu.CompilerParams(vmem_limit_bytes=8 * 2**20)
CHUNK = dict(
    compiler_params=pltpu.CompilerParams(vmem_limit_bytes=16 * 2**20),
    cost_estimate=pl.CostEstimate(flops=45 * 10**8, bytes_accessed=4 * 10**6, transcendentals=0),
)


def away(rows, cols, pan, pdeg):
    return pl.pallas_call(
        away_kernel,
        out_shape=jax.ShapeDtypeStruct((4, MSG, 128), BF16),
        in_specs=[VMEM] * 5,
        out_specs=VMEM,
        name="tile_away",
        **CHUNK,
    )(rows, *cols, pan, pdeg)


def first_kernel(where_ref, rows_ref, c0_ref, c1_ref, zp_ref, pan_ref, pdeg_ref, send_ref):
    panel_kernel(where_ref, c0_ref, c1_ref, zp_ref, pan_ref, pdeg_ref)
    away_kernel(rows_ref, c0_ref, c1_ref, pan_ref, pdeg_ref, send_ref)


def first(where, rows, cols, zp):
    return pl.pallas_call(
        first_kernel,
        out_shape=[
            jax.ShapeDtypeStruct((4096, 256), BF16),
            jax.ShapeDtypeStruct((8, 128), F32),
            jax.ShapeDtypeStruct((4, MSG, 128), BF16),
        ],
        in_specs=[SMEM] + [VMEM] * 4,
        out_specs=[VMEM] * 3,
        name="tile_first",
        **CHUNK,
    )(where, rows, *cols, zp)


def home_kernel(rows_ref, c0_ref, c1_ref, pan_ref, sum_ref, deg_ref):
    acc = chunk_sums(rows_ref, c0_ref, c1_ref, pan_ref, True)
    sum_ref[...] = acc[:, :128]
    deg_ref[...] = jnp.concatenate(sum([degree_rows(acc, k) for k in range(4)], []), axis=0)


def home(rows, cols, pan):
    return pl.pallas_call(
        home_kernel,
        out_shape=[jax.ShapeDtypeStruct((1024, 128), F32), jax.ShapeDtypeStruct((8, 128), F32)],
        in_specs=[VMEM] * 4,
        out_specs=[VMEM, VMEM],
        name="tile_home",
        **CHUNK,
    )(rows, *cols, pan)


def combine_kernel(home_ref, deg_ref, pdeg_ref, g0, g1, g2, sum_ref, *sends):
    degrees = []
    pdeg = pdeg_ref[0:1, :]
    for k in range(4):
        p = home_ref[k * 256 : k * 256 + 256, :]
        d = deg_ref[k * 2 : k * 2 + 2, :]
        for g in (g0, g1, g2):
            p = p + g[k, :256, :].astype(F32)
            t = g[k, 256:264, :].astype(F32) + g[k, 264:272, :].astype(F32)
            d = d + t[0:2]
            if k == 0:
                pdeg = pdeg + t[2:3]
        if k == 0:
            sum_ref[:256, :] = p
        else:
            sends[k - 1][:256, :] = p.astype(BF16)
        degrees.append(d)
    for k in range(4):
        turned = [degrees[(k + i) % 4] for i in range(4)]
        tail = jnp.concatenate(turned + [pdeg, jnp.zeros((7, 128), F32)], axis=0)
        if k == 0:
            sum_ref[256:, :] = tail
        else:
            sends[k - 1][256:, :] = split_rows(tail)


def combine(products, degrees, pdeg, gots):
    return pl.pallas_call(
        combine_kernel,
        out_shape=[jax.ShapeDtypeStruct((272, 128), F32)] + [jax.ShapeDtypeStruct((LAST, 128), BF16)] * 3,
        in_specs=[VMEM] * 6,
        out_specs=[VMEM] * 4,
        name="combine",
        compiler_params=SMALL,
    )(products, degrees, pdeg, *gots)


def finish_kernel(sum_ref, g0, g1, g2, total_ref, top_ref):
    p, t = sum_ref[:256, :], sum_ref[256:, :]
    for g in (g0, g1, g2):
        p = p + g[:256, :].astype(F32)
        t = t + (g[256:272, :].astype(F32) + g[272:288, :].astype(F32))
    total_ref[:256, :] = p
    total_ref[256:, :] = t
    top_ref[...] = jnp.broadcast_to(jnp.max(t[0:8], keepdims=True)[None], top_ref.shape)


def finish(own, gots):
    return pl.pallas_call(
        finish_kernel,
        out_shape=[jax.ShapeDtypeStruct((272, 128), F32), jax.ShapeDtypeStruct((PEERS, 8, 128), F32)],
        in_specs=[VMEM] * 4,
        out_specs=[VMEM, VMEM],
        name="finish",
        compiler_params=SMALL,
    )(own, *gots)


def correlation_kernel(where_ref, total_ref, block_ref, zp_ref, out_ref):
    zp = zp_ref[...]
    r = lax.broadcasted_iota(jnp.int32, (128, 128), 0)
    c = lax.broadcasted_iota(jnp.int32, (128, 128), 1)
    for half in range(2):
        rows = slice(half * 128, half * 128 + 128)
        direct = sixth(lax.dot_general(block_ref[rows, :], zp, ROWS_T, preferred_element_type=F32))
        same = (r == c) & (where_ref[0] == half)
        direct = jnp.where(same, 0.0, direct)
        degree = jnp.broadcast_to(total_ref[256 + half : 257 + half, :], (128, 128)).T
        lower = jnp.minimum(degree, total_ref[264:265, :])
        value = (total_ref[rows, :] + direct) / (lower + 1.0 - direct)
        out_ref[rows, :] = jnp.where(same, 1.0, value)


def correlate(where, total, block, zp):
    return pl.pallas_call(
        correlation_kernel,
        out_shape=jax.ShapeDtypeStruct((256, 128), F32),
        in_specs=[SMEM] + [VMEM] * 3,
        out_specs=VMEM,
        name="correlate",
        compiler_params=SMALL,
    )(where, total, block, zp)


def scale_kernel(total_ref, tops_ref, out_ref):
    out_ref[...] = total_ref[256:258, :] / jnp.max(tops_ref[...], axis=0)[0:2]


def scale(total, tops):
    return pl.pallas_call(
        scale_kernel,
        out_shape=jax.ShapeDtypeStruct((2, 128), F32),
        in_specs=[VMEM] * 2,
        out_specs=VMEM,
        name="scale",
        compiler_params=SMALL,
    )(total, tops)


def pick(parts, index):
    out = parts[0]
    for k in range(1, len(parts)):
        out = jnp.where(index == k, parts[k], out)
    return out


def on_device(expression, panel_index):
    at = {a: lax.axis_index(a) for a in AXES}
    block = standardize(expression)

    half = panel_index[0] % 2
    rest = panel_index[0] // 2
    far = {}
    for a in reversed(AXES):
        far[a] = (rest % SIZES[a] - at[a]) % SIZES[a]
        rest = rest // SIZES[a]
    place = far["y"] * 4 + far["zl"] * 2 + half
    here = (far["x"] == 0) & (far["zh"] == 0)
    where = jnp.where(here, far["core"] * 16 + place, -1).astype(jnp.int32)[None]

    pair = jnp.concatenate(ring(block, "zl"))
    group = jnp.concatenate(ring(block, "zh"))
    near = jnp.concatenate(ring(pair, "y"))
    right, left = recv(group, "x", 1), recv(group, "x", 3)
    near, group = lax.optimization_barrier((near, group))

    zp = lax.dynamic_slice_in_dim(near, place * 128, 128, 0)
    zp = pick(ring(zp, "core"), far["core"])
    zp, near = lax.optimization_barrier((zp, near))
    cols = (near, recv(near, "core", 1))
    zp = pick(ring(zp, "zh"), far["zh"])
    zp, right, left = lax.optimization_barrier((zp, right, left))
    apart = recv(right[:512], "x", 1), recv(left[512:], "x", 3)
    zp = pick(ring(zp, "x"), far["x"])

    pan, pdeg, part = first(where, right, cols, zp)
    gots = [recv(part, "x", 3)]
    near_half, far_half, part = lax.optimization_barrier((*apart, part))
    part = away(jnp.concatenate([near_half, far_half]), cols, pan, pdeg)
    gots.append(recv(part, "x", 2))
    part = away(after(left, part, gots[0]), cols, pan, pdeg)
    gots.append(recv(part, "x", 1))
    own, degrees = home(after(group, part), cols, pan)
    mine, *sends = combine(own, degrees, pdeg, gots)
    total, top = finish(mine, [recv(sends[k - 1], "zh", 4 - k) for k in (1, 2, 3)])
    tops = lax.all_to_all(top, PEER_AXES, 0, 0)
    correlation = correlate(where, total, block, zp)
    return (scale(total, tops).reshape(256), correlation)


def solution(mesh):
    inner = Mesh(mesh.devices.reshape([SIZES[a] for a in AXES]), AXES)
    return jax.shard_map(
        on_device,
        mesh=inner,
        in_specs=(P(AXES, None), P()),
        out_specs=(P(AXES), P(AXES, None)),
        check_vma=False,
    )
```

```python
import jax
import jax.numpy as jnp
from jax import lax
from jax.experimental import pallas as pl
from jax.experimental.pallas import tpu as pltpu
from jax.sharding import Mesh
from jax.sharding import PartitionSpec as P

AXES = ("zl", "y", "core", "zh", "x")
SIZES = {"zl": 2, "y": 4, "core": 2, "zh": 4, "x": 4}
ROWS_T = (((1,), (1,)), ((), ()))
F32 = jnp.float32
BF16 = jnp.bfloat16
VMEM = pl.BlockSpec(memory_space=pltpu.VMEM)
SMEM = pl.BlockSpec(memory_space=pltpu.SMEM)
MSG = 272
LAST = 288
PEER_AXES = ("zl", "y", "core", "x")
PEERS = 64


def recv(value, axis, delta):
    size = SIZES[axis]
    return lax.ppermute(value, axis, [((i + delta) % size, i) for i in range(size)])


def ring(value, axis):
    return [value] + [recv(value, axis, d) for d in range(1, SIZES[axis])]


def after(value, *others):
    return lax.optimization_barrier((value, *others))[0]


def sixth(c):
    s = c * c
    return s * s * s


def split_rows(v):
    hi = v.astype(BF16).astype(F32)
    return jnp.concatenate([hi, v - hi], axis=0).astype(BF16)


def standardize_kernel(x_ref, out_ref):
    values = x_ref[...].astype(F32)
    center = values - jnp.mean(values, axis=1, keepdims=True)
    spread = jnp.mean(center * center, axis=1, keepdims=True)
    out_ref[...] = (center * lax.rsqrt(spread + 1e-05)).astype(BF16) * BF16(0.0625)


def standardize(x):
    return pl.pallas_call(
        standardize_kernel,
        out_shape=jax.ShapeDtypeStruct(x.shape, BF16),
        in_specs=[VMEM],
        out_specs=VMEM,
        name="standardize",
        compiler_params=SMALL,
    )(x)


def panel_kernel(where_ref, c0_ref, c1_ref, zp_ref, pan_ref, pdeg_ref):
    zp = zp_ref[...]
    total = jnp.zeros((1, 128), F32)
    r = lax.broadcasted_iota(jnp.int32, (512, 128), 0)
    c = lax.broadcasted_iota(jnp.int32, (512, 128), 1)
    for g in range(8):
        rows = (c0_ref, c1_ref)[g // 4][(g % 4) * 512 : (g % 4) * 512 + 512, :]
        v = sixth(lax.dot_general(rows, zp, ROWS_T, preferred_element_type=F32))
        v = jnp.where(r + g * 512 == c + where_ref[0] * 128, 0.0, v)
        total = total + jnp.sum(v, axis=0, keepdims=True)
        pan_ref[g * 512 : g * 512 + 512, :128] = v.astype(BF16)
    pan_ref[:, 128:] = jnp.ones((4096, 128), BF16)
    pdeg_ref[...] = jnp.broadcast_to(total, (8, 128))


def chunk_sums(rows_ref, c0_ref, c1_ref, pan_ref, scratch, own):
    rows = rows_ref[...]
    for j in range(16):
        zc = (c0_ref, c1_ref)[j // 8][(j % 8) * 256 : (j % 8) * 256 + 256, :]
        a = sixth(lax.dot_general(rows, zc, ROWS_T, preferred_element_type=F32))
        if own and j == 0:
            gene = lax.broadcasted_iota(jnp.int32, a.shape, 0)
            a = jnp.where(gene == lax.broadcasted_iota(jnp.int32, a.shape, 1), 0.0, a)
        scratch[:, j * 256 : j * 256 + 256] = a.astype(BF16)
    return jnp.dot(scratch[...], pan_ref[...], preferred_element_type=F32)


def degree_rows(acc, k):
    flat = acc[k * 256 : k * 256 + 256, 128:]
    return [flat[:128].T[0:1], flat[128:].T[0:1]]


def away_kernel(rows_ref, c0_ref, c1_ref, pan_ref, pdeg_ref, send_ref, scratch):
    acc = chunk_sums(rows_ref, c0_ref, c1_ref, pan_ref, scratch, False)
    for k in range(4):
        send_ref[k, :256, :] = acc[k * 256 : k * 256 + 256, :128].astype(BF16)
        tail = jnp.concatenate(degree_rows(acc, k) + [pdeg_ref[0:1, :], jnp.zeros((5, 128), F32)], axis=0)
        send_ref[k, 256:, :] = split_rows(tail)


SMALL = pltpu.CompilerParams(vmem_limit_bytes=8 * 2**20)
CHUNK = dict(
    scratch_shapes=[pltpu.VMEM((1024, 4096), BF16)],
    compiler_params=pltpu.CompilerParams(vmem_limit_bytes=24 * 2**20),
    cost_estimate=pl.CostEstimate(flops=45 * 10**8, bytes_accessed=4 * 10**6, transcendentals=0),
)


def away(rows, cols, pan, pdeg):
    return pl.pallas_call(
        away_kernel,
        out_shape=jax.ShapeDtypeStruct((4, MSG, 128), BF16),
        in_specs=[VMEM] * 5,
        out_specs=VMEM,
        name="tile_away",
        **CHUNK,
    )(rows, *cols, pan, pdeg)


def first_kernel(where_ref, rows_ref, c0_ref, c1_ref, zp_ref, pan_ref, pdeg_ref, kept_ref, send_ref, scratch):
    panel_kernel(where_ref, c0_ref, c1_ref, zp_ref, pan_ref, pdeg_ref)
    kept_ref[...] = c1_ref[...]
    away_kernel(rows_ref, c0_ref, c1_ref, pan_ref, pdeg_ref, send_ref, scratch)


def first(where, rows, cols, zp):
    return pl.pallas_call(
        first_kernel,
        out_shape=[
            jax.ShapeDtypeStruct((4096, 256), BF16),
            jax.ShapeDtypeStruct((8, 128), F32),
            jax.ShapeDtypeStruct((2048, 256), BF16),
            jax.ShapeDtypeStruct((4, MSG, 128), BF16),
        ],
        in_specs=[SMEM] + [VMEM] * 4,
        out_specs=[VMEM] * 4,
        name="tile_first",
        **CHUNK,
    )(where, rows, *cols, zp)


def home_kernel(rows_ref, c0_ref, c1_ref, pan_ref, sum_ref, deg_ref, scratch):
    acc = chunk_sums(rows_ref, c0_ref, c1_ref, pan_ref, scratch, True)
    sum_ref[...] = acc[:, :128]
    deg_ref[...] = jnp.concatenate(sum([degree_rows(acc, k) for k in range(4)], []), axis=0)


def home(rows, cols, pan):
    return pl.pallas_call(
        home_kernel,
        out_shape=[jax.ShapeDtypeStruct((1024, 128), F32), jax.ShapeDtypeStruct((8, 128), F32)],
        in_specs=[VMEM] * 4,
        out_specs=[VMEM, VMEM],
        name="tile_home",
        **CHUNK,
    )(rows, *cols, pan)


def combine_kernel(home_ref, deg_ref, pdeg_ref, g0, g1, g2, sum_ref, *sends):
    degrees = []
    pdeg = pdeg_ref[0:1, :]
    for k in range(4):
        p = home_ref[k * 256 : k * 256 + 256, :]
        d = deg_ref[k * 2 : k * 2 + 2, :]
        for g in (g0, g1, g2):
            p = p + g[k, :256, :].astype(F32)
            t = g[k, 256:264, :].astype(F32) + g[k, 264:272, :].astype(F32)
            d = d + t[0:2]
            if k == 0:
                pdeg = pdeg + t[2:3]
        if k == 0:
            sum_ref[:256, :] = p
        else:
            sends[k - 1][:256, :] = p.astype(BF16)
        degrees.append(d)
    for k in range(4):
        turned = [degrees[(k + i) % 4] for i in range(4)]
        tail = jnp.concatenate(turned + [pdeg, jnp.zeros((7, 128), F32)], axis=0)
        if k == 0:
            sum_ref[256:, :] = tail
        else:
            sends[k - 1][256:, :] = split_rows(tail)


def combine(products, degrees, pdeg, gots):
    return pl.pallas_call(
        combine_kernel,
        out_shape=[jax.ShapeDtypeStruct((272, 128), F32)] + [jax.ShapeDtypeStruct((LAST, 128), BF16)] * 3,
        in_specs=[VMEM] * 6,
        out_specs=[VMEM] * 4,
        name="combine",
        compiler_params=SMALL,
    )(products, degrees, pdeg, *gots)


def finish_kernel(sum_ref, g0, g1, g2, total_ref, top_ref):
    p, t = sum_ref[:256, :], sum_ref[256:, :]
    for g in (g0, g1, g2):
        p = p + g[:256, :].astype(F32)
        t = t + (g[256:272, :].astype(F32) + g[272:288, :].astype(F32))
    total_ref[:256, :] = p
    total_ref[256:, :] = t
    top_ref[...] = jnp.broadcast_to(jnp.max(t[0:8], keepdims=True)[None], top_ref.shape)


def finish(own, gots):
    return pl.pallas_call(
        finish_kernel,
        out_shape=[jax.ShapeDtypeStruct((272, 128), F32), jax.ShapeDtypeStruct((PEERS, 1, 128), F32)],
        in_specs=[VMEM] * 4,
        out_specs=[VMEM, VMEM],
        name="finish",
        compiler_params=SMALL,
    )(own, *gots)


def correlation_kernel(where_ref, total_ref, block_ref, zp_ref, out_ref):
    zp = zp_ref[...]
    r = lax.broadcasted_iota(jnp.int32, (128, 128), 0)
    c = lax.broadcasted_iota(jnp.int32, (128, 128), 1)
    for half in range(2):
        rows = slice(half * 128, half * 128 + 128)
        direct = sixth(lax.dot_general(block_ref[rows, :], zp, ROWS_T, preferred_element_type=F32))
        same = (r == c) & (where_ref[0] == half)
        direct = jnp.where(same, 0.0, direct)
        degree = jnp.broadcast_to(total_ref[256 + half : 257 + half, :], (128, 128)).T
        lower = jnp.minimum(degree, total_ref[264:265, :])
        value = (total_ref[rows, :] + direct) / (lower + 1.0 - direct)
        out_ref[rows, :] = jnp.where(same, 1.0, value)


def correlate(where, total, block, zp):
    return pl.pallas_call(
        correlation_kernel,
        out_shape=jax.ShapeDtypeStruct((256, 128), F32),
        in_specs=[SMEM] + [VMEM] * 3,
        out_specs=VMEM,
        name="correlate",
        compiler_params=SMALL,
    )(where, total, block, zp)


def scale_kernel(total_ref, tops_ref, out_ref):
    out_ref[...] = total_ref[256:258, :] / jnp.max(tops_ref[...], axis=0)


def scale(total, tops):
    return pl.pallas_call(
        scale_kernel,
        out_shape=jax.ShapeDtypeStruct((2, 128), F32),
        in_specs=[VMEM] * 2,
        out_specs=VMEM,
        name="scale",
        compiler_params=SMALL,
    )(total, tops)


def pick(parts, index):
    out = parts[0]
    for k in range(1, len(parts)):
        out = jnp.where(index == k, parts[k], out)
    return out


def on_device(expression, panel_index):
    at = {a: lax.axis_index(a) for a in AXES}
    block = standardize(expression)

    half = panel_index[0] % 2
    rest = panel_index[0] // 2
    far = {}
    for a in reversed(AXES):
        far[a] = (rest % SIZES[a] - at[a]) % SIZES[a]
        rest = rest // SIZES[a]
    place = far["y"] * 4 + far["zl"] * 2 + half
    here = (far["x"] == 0) & (far["zh"] == 0)
    where = jnp.where(here, far["core"] * 16 + place, -1).astype(jnp.int32)[None]

    pair = jnp.concatenate(ring(block, "zl"))
    group = jnp.concatenate(ring(block, "zh"))
    near = jnp.concatenate(ring(pair, "y"))
    right, left = recv(group, "x", 1), recv(group, "x", 3)
    near, group = lax.optimization_barrier((near, group))

    zp = lax.dynamic_slice_in_dim(near, place * 128, 128, 0)
    zp = pick(ring(zp, "core"), far["core"])
    zp, near = lax.optimization_barrier((zp, near))
    cols = (near, recv(near, "core", 1))
    zp = pick(ring(zp, "zh"), far["zh"])
    zp, right, left = lax.optimization_barrier((zp, right, left))
    apart = recv(right[:512], "x", 1), recv(left[512:], "x", 3)
    zp = pick(ring(zp, "x"), far["x"])

    pan, pdeg, kept, part = first(where, right, cols, zp)
    cols = (near, kept)
    gots = [recv(part, "x", 3)]
    near_half, far_half, part = lax.optimization_barrier((*apart, part))
    part = away(jnp.concatenate([near_half, far_half]), cols, pan, pdeg)
    gots.append(recv(part, "x", 2))
    part = away(after(left, part), cols, pan, pdeg)
    gots.append(recv(part, "x", 1))
    own, degrees = home(after(group, part, gots[0]), cols, pan)
    mine, *sends = combine(own, degrees, pdeg, gots)
    total, top = finish(mine, [recv(sends[k - 1], "zh", 4 - k) for k in (1, 2, 3)])
    tops = lax.all_to_all(top, PEER_AXES, 0, 0)
    correlation = correlate(where, total, block, zp)
    return (scale(total, tops).reshape(256), correlation)


def solution(mesh):
    inner = Mesh(mesh.devices.reshape([SIZES[a] for a in AXES]), AXES)
    return jax.shard_map(
        on_device,
        mesh=inner,
        in_specs=(P(AXES, None), P()),
        out_specs=(P(AXES), P(AXES, None)),
        check_vma=False,
    )
```

```python
import jax
import jax.numpy as jnp
from jax import lax
from jax.experimental import pallas as pl
from jax.experimental.pallas import tpu as pltpu
from jax.sharding import Mesh
from jax.sharding import PartitionSpec as P

AXES = ("zl", "y", "core", "zh", "x")
SIZES = {"zl": 2, "y": 4, "core": 2, "zh": 4, "x": 4}
ROWS_T = (((1,), (1,)), ((), ()))
F32 = jnp.float32
BF16 = jnp.bfloat16
VMEM = pl.BlockSpec(memory_space=pltpu.VMEM)
SMEM = pl.BlockSpec(memory_space=pltpu.SMEM)
MSG = 272
LAST = 288
PEER_AXES = ("zl", "y", "core", "x")
PEERS = 64


def recv(value, axis, delta):
    size = SIZES[axis]
    return lax.ppermute(value, axis, [((i + delta) % size, i) for i in range(size)])


def ring(value, axis):
    found = {0: value}
    for d in (1, 3, 2):
        if d < SIZES[axis]:
            found[d] = recv(value, axis, d)
    return [found[d] for d in range(SIZES[axis])]


def after(value, *others):
    return lax.optimization_barrier((value, *others))[0]


def sixth(c):
    s = c * c
    return s * s * s


def split_rows(v):
    hi = v.astype(BF16).astype(F32)
    return jnp.concatenate([hi, v - hi], axis=0).astype(BF16)


def standardize_kernel(x_ref, out_ref):
    values = x_ref[...].astype(F32)
    center = values - jnp.mean(values, axis=1, keepdims=True)
    spread = jnp.mean(center * center, axis=1, keepdims=True)
    out_ref[...] = (center * lax.rsqrt(spread + 1e-05)).astype(BF16) * BF16(0.0625)


def standardize(x):
    return pl.pallas_call(
        standardize_kernel,
        out_shape=jax.ShapeDtypeStruct(x.shape, BF16),
        in_specs=[VMEM],
        out_specs=VMEM,
        name="standardize",
        compiler_params=SMALL,
    )(x)


def panel_kernel(where_ref, c0_ref, c1_ref, zp_ref, pan_ref, pdeg_ref):
    zp = zp_ref[...]
    total = jnp.zeros((1, 128), F32)
    r = lax.broadcasted_iota(jnp.int32, (512, 128), 0)
    c = lax.broadcasted_iota(jnp.int32, (512, 128), 1)
    for g in range(8):
        rows = (c0_ref, c1_ref)[g // 4][(g % 4) * 512 : (g % 4) * 512 + 512, :]
        v = sixth(lax.dot_general(rows, zp, ROWS_T, preferred_element_type=F32))
        v = jnp.where(r + g * 512 == c + where_ref[0] * 128, 0.0, v)
        total = total + jnp.sum(v, axis=0, keepdims=True)
        pan_ref[g * 512 : g * 512 + 512, :128] = v.astype(BF16)
    pan_ref[:, 128:] = jnp.ones((4096, 128), BF16)
    pdeg_ref[...] = jnp.broadcast_to(total, (8, 128))


def chunk_sums(rows_ref, c0_ref, c1_ref, pan_ref, scratch, own):
    rows = rows_ref[...]
    for j in range(16):
        zc = (c0_ref, c1_ref)[j // 8][(j % 8) * 256 : (j % 8) * 256 + 256, :]
        a = sixth(lax.dot_general(rows, zc, ROWS_T, preferred_element_type=F32))
        if own and j == 0:
            gene = lax.broadcasted_iota(jnp.int32, a.shape, 0)
            a = jnp.where(gene == lax.broadcasted_iota(jnp.int32, a.shape, 1), 0.0, a)
        scratch[:, j * 256 : j * 256 + 256] = a.astype(BF16)
    return jnp.dot(scratch[...], pan_ref[...], preferred_element_type=F32)


def degree_rows(acc, k):
    flat = acc[k * 256 : k * 256 + 256, 128:]
    return [flat[:128].T[0:1], flat[128:].T[0:1]]


def away_kernel(rows_ref, c0_ref, c1_ref, pan_ref, pdeg_ref, send_ref, scratch):
    acc = chunk_sums(rows_ref, c0_ref, c1_ref, pan_ref, scratch, False)
    for k in range(4):
        send_ref[k, :256, :] = acc[k * 256 : k * 256 + 256, :128].astype(BF16)
        tail = jnp.concatenate(degree_rows(acc, k) + [pdeg_ref[0:1, :], jnp.zeros((5, 128), F32)], axis=0)
        send_ref[k, 256:, :] = split_rows(tail)


SMALL = pltpu.CompilerParams(vmem_limit_bytes=8 * 2**20)
CHUNK = dict(
    scratch_shapes=[pltpu.VMEM((1024, 4096), BF16)],
    compiler_params=pltpu.CompilerParams(vmem_limit_bytes=24 * 2**20),
    cost_estimate=pl.CostEstimate(flops=45 * 10**8, bytes_accessed=4 * 10**6, transcendentals=0),
)


def away(rows, cols, pan, pdeg):
    return pl.pallas_call(
        away_kernel,
        out_shape=jax.ShapeDtypeStruct((4, MSG, 128), BF16),
        in_specs=[VMEM] * 5,
        out_specs=VMEM,
        name="tile_away",
        **CHUNK,
    )(rows, *cols, pan, pdeg)


def first_kernel(where_ref, rows_ref, c0_ref, ca_ref, cb_ref, zp_ref, pan_ref, pdeg_ref, kept_ref, send_ref, scratch):
    kept_ref[:1024, :] = ca_ref[...]
    kept_ref[1024:, :] = cb_ref[...]
    panel_kernel(where_ref, c0_ref, kept_ref, zp_ref, pan_ref, pdeg_ref)
    away_kernel(rows_ref, c0_ref, kept_ref, pan_ref, pdeg_ref, send_ref, scratch)


def first(where, rows, cols, zp):
    return pl.pallas_call(
        first_kernel,
        out_shape=[
            jax.ShapeDtypeStruct((4096, 256), BF16),
            jax.ShapeDtypeStruct((8, 128), F32),
            jax.ShapeDtypeStruct((2048, 256), BF16),
            jax.ShapeDtypeStruct((4, MSG, 128), BF16),
        ],
        in_specs=[SMEM] + [VMEM] * 5,
        out_specs=[VMEM] * 4,
        name="tile_first",
        **CHUNK,
    )(where, rows, *cols, zp)


def home_kernel(rows_ref, c0_ref, c1_ref, pan_ref, sum_ref, deg_ref, scratch):
    acc = chunk_sums(rows_ref, c0_ref, c1_ref, pan_ref, scratch, True)
    sum_ref[...] = acc[:, :128]
    deg_ref[...] = jnp.concatenate(sum([degree_rows(acc, k) for k in range(4)], []), axis=0)


def home(rows, cols, pan):
    return pl.pallas_call(
        home_kernel,
        out_shape=[jax.ShapeDtypeStruct((1024, 128), F32), jax.ShapeDtypeStruct((8, 128), F32)],
        in_specs=[VMEM] * 4,
        out_specs=[VMEM, VMEM],
        name="tile_home",
        **CHUNK,
    )(rows, *cols, pan)


def combine_kernel(home_ref, deg_ref, pdeg_ref, g0, g1, g2, sum_ref, *sends):
    degrees = []
    pdeg = pdeg_ref[0:1, :]
    for k in range(4):
        p = home_ref[k * 256 : k * 256 + 256, :]
        d = deg_ref[k * 2 : k * 2 + 2, :]
        for g in (g0, g1, g2):
            p = p + g[k, :256, :].astype(F32)
            t = g[k, 256:264, :].astype(F32) + g[k, 264:272, :].astype(F32)
            d = d + t[0:2]
            if k == 0:
                pdeg = pdeg + t[2:3]
        if k == 0:
            sum_ref[:256, :] = p
        else:
            sends[k - 1][:256, :] = p.astype(BF16)
        degrees.append(d)
    for k in range(4):
        turned = [degrees[(k + i) % 4] for i in range(4)]
        tail = jnp.concatenate(turned + [pdeg, jnp.zeros((7, 128), F32)], axis=0)
        if k == 0:
            sum_ref[256:, :] = tail
        else:
            sends[k - 1][256:, :] = split_rows(tail)


def combine(products, degrees, pdeg, gots):
    return pl.pallas_call(
        combine_kernel,
        out_shape=[jax.ShapeDtypeStruct((272, 128), F32)] + [jax.ShapeDtypeStruct((LAST, 128), BF16)] * 3,
        in_specs=[VMEM] * 6,
        out_specs=[VMEM] * 4,
        name="combine",
        compiler_params=SMALL,
    )(products, degrees, pdeg, *gots)


def finish_kernel(sum_ref, g0, g1, g2, total_ref, top_ref):
    p, t = sum_ref[:256, :], sum_ref[256:, :]
    for g in (g0, g1, g2):
        p = p + g[:256, :].astype(F32)
        t = t + (g[256:272, :].astype(F32) + g[272:288, :].astype(F32))
    total_ref[:256, :] = p
    total_ref[256:, :] = t
    top_ref[...] = jnp.broadcast_to(jnp.max(t[0:8], keepdims=True)[None], top_ref.shape)


def finish(own, gots):
    return pl.pallas_call(
        finish_kernel,
        out_shape=[jax.ShapeDtypeStruct((272, 128), F32), jax.ShapeDtypeStruct((PEERS, 1, 128), F32)],
        in_specs=[VMEM] * 4,
        out_specs=[VMEM, VMEM],
        name="finish",
        compiler_params=SMALL,
    )(own, *gots)


def correlation_kernel(where_ref, total_ref, block_ref, zp_ref, out_ref):
    zp = zp_ref[...]
    r = lax.broadcasted_iota(jnp.int32, (128, 128), 0)
    c = lax.broadcasted_iota(jnp.int32, (128, 128), 1)
    for half in range(2):
        rows = slice(half * 128, half * 128 + 128)
        direct = sixth(lax.dot_general(block_ref[rows, :], zp, ROWS_T, preferred_element_type=F32))
        same = (r == c) & (where_ref[0] == half)
        direct = jnp.where(same, 0.0, direct)
        degree = jnp.broadcast_to(total_ref[256 + half : 257 + half, :], (128, 128)).T
        lower = jnp.minimum(degree, total_ref[264:265, :])
        value = (total_ref[rows, :] + direct) / (lower + 1.0 - direct)
        out_ref[rows, :] = jnp.where(same, 1.0, value)


def correlate(where, total, block, zp):
    return pl.pallas_call(
        correlation_kernel,
        out_shape=jax.ShapeDtypeStruct((256, 128), F32),
        in_specs=[SMEM] + [VMEM] * 3,
        out_specs=VMEM,
        name="correlate",
        compiler_params=SMALL,
    )(where, total, block, zp)


def scale_kernel(total_ref, tops_ref, out_ref):
    out_ref[...] = total_ref[256:258, :] / jnp.max(tops_ref[...], axis=0)


def scale(total, tops):
    return pl.pallas_call(
        scale_kernel,
        out_shape=jax.ShapeDtypeStruct((2, 128), F32),
        in_specs=[VMEM] * 2,
        out_specs=VMEM,
        name="scale",
        compiler_params=SMALL,
    )(total, tops)


def pick(parts, index):
    out = parts[0]
    for k in range(1, len(parts)):
        out = jnp.where(index == k, parts[k], out)
    return out


def on_device(expression, panel_index):
    at = {a: lax.axis_index(a) for a in AXES}
    block = standardize(expression)

    half = panel_index[0] % 2
    rest = panel_index[0] // 2
    far = {}
    for a in reversed(AXES):
        far[a] = (rest % SIZES[a] - at[a]) % SIZES[a]
        rest = rest // SIZES[a]
    place = far["y"] * 4 + far["zl"] * 2 + half
    here = (far["x"] == 0) & (far["zh"] == 0)
    where = jnp.where(here, far["core"] * 16 + place, -1).astype(jnp.int32)[None]

    pair = jnp.concatenate(ring(block, "zl"))
    group = jnp.concatenate(ring(block, "zh"))
    near = jnp.concatenate(ring(pair, "y"))
    right, left = recv(group, "x", 1), recv(group, "x", 3)
    near, group = lax.optimization_barrier((near, group))

    zp = lax.dynamic_slice_in_dim(near, place * 128, 128, 0)
    zp = pick(ring(zp, "core"), far["core"])
    zp, near = lax.optimization_barrier((zp, near))
    cols = (near, recv(near[:1024], "core", 1), recv(near[1024:], "core", 1))
    zp = pick(ring(zp, "zh"), far["zh"])
    zp, right, left = lax.optimization_barrier((zp, right, left))
    apart = recv(right[:512], "x", 1), recv(left[512:], "x", 3)
    zp = pick(ring(zp, "x"), far["x"])

    pan, pdeg, kept, part = first(where, right, cols, zp)
    cols = (near, kept)
    gots = [recv(part, "x", 3)]
    near_half, far_half, part = lax.optimization_barrier((*apart, part))
    part = away(jnp.concatenate([near_half, far_half]), cols, pan, pdeg)
    gots.append(recv(part, "x", 2))
    part = away(after(left, part), cols, pan, pdeg)
    gots.append(recv(part, "x", 1))
    own, degrees = home(after(group, part, gots[0]), cols, pan)
    mine, *sends = combine(own, degrees, pdeg, gots)
    total, top = finish(mine, [recv(sends[k - 1], "zh", 4 - k) for k in (2, 1, 3)])
    tops = lax.all_to_all(top, PEER_AXES, 0, 0)
    correlation = correlate(where, total, block, zp)
    return (scale(total, tops).reshape(256), correlation)


def solution(mesh):
    inner = Mesh(mesh.devices.reshape([SIZES[a] for a in AXES]), AXES)
    return jax.shard_map(
        on_device,
        mesh=inner,
        in_specs=(P(AXES, None), P()),
        out_specs=(P(AXES), P(AXES, None)),
        check_vma=False,
    )
```
